1024 devices in a mesh: expert: 16 (over y, core), replica: 64 (over x, z).
Axes of the slice: x: 4, y: 8, z: 16, core: 2. Of those that a mesh axis runs over, the one named last changes fastest.
Arguments:
- hidden_in: bfloat16 [1024, 3584], P('replica'), may hold values from -6 to 6
- norm_gain: float32 [3584], replicated, may hold values from 0.5 to 1.5
- expert_ids: int32 [1024, 8], P('replica'), may hold values from 0 to 63, all different within a row; in each aligned block of 16 rows (0 to 15, 16 to 31, ...) at most 4 rows name the same one
- gate_scores: int32 [1024, 8], P('replica'), may hold values from 1 to 64
- w_gate: bfloat16 [64, 1024, 3584], P('replica', 'expert'), may hold values from -0.09375 to 0.09375
- w_up: bfloat16 [64, 1024, 3584], P('replica', 'expert'), may hold values from -0.09375 to 0.09375
- w_down: bfloat16 [64, 1024, 3584], P('replica', 'expert'), may hold values from -0.1875 to 0.1875
- shared_gate: bfloat16 [1024, 3584], P('expert'), may hold values from -0.09375 to 0.09375
- shared_up: bfloat16 [1024, 3584], P('expert'), may hold values from -0.09375 to 0.09375
- shared_down: bfloat16 [1024, 3584], P('expert'), may hold values from -0.1875 to 0.1875
- out_grad: bfloat16 [1024, 3584], P('replica'), may hold values from -6 to 6
Outputs:
- moe_out: bfloat16 [1024, 3584], P('replica')
- hidden_grad: bfloat16 [1024, 3584], P('replica')
- gain_grad: float32 [3584], P('replica')
- gate_grad: bfloat16 [64, 1024, 3584], P('replica', 'expert')
- up_grad: bfloat16 [64, 1024, 3584], P('replica', 'expert')
- down_grad: bfloat16 [64, 1024, 3584], P('replica', 'expert')
- shared_gate_grad: bfloat16 [1024, 3584], P('expert', 'replica')
- shared_up_grad: bfloat16 [1024, 3584], P('expert', 'replica')
- shared_down_grad: bfloat16 [1024, 3584], P('expert', 'replica')
The draws below stay inside these ranges and needn't reach their ends.
Inputs may be any that keep to these rules, and one draw needn't show every extreme that they name: `expert_ids`: each row names 8 different experts; within the rows of one replica index (aligned blocks of 16 rows) no expert is named more than 4 times, a bound that some block reaches.
All inputs are finite; a program needn't handle non-finite values.
Results may differ from the reference program's by a relative error of at most 0.024.
Values may be sent and summed in bfloat16 or wider, within the bound.
A program may use at most 64 MiB of HBM per device.

```python
import math
import jax
import jax.numpy as jnp
import numpy as np
from jax import lax

D = 3584
FF = 1024
TOP = 8
TOK_REP = 16
EXPERTS = 64
CAP = 4
TOKENS = 1024
N_EXPERT = 16
N_REPLICA = 64


def touch_ends(drawn, key, smallest, high):
    longest = drawn.shape.index(max(drawn.shape))
    spots = []
    for shift in (0, 1):
        where = [jax.random.randint(jax.random.fold_in(key, axis), (), 0, length) for axis, length in enumerate(drawn.shape)]
        where[longest] = (where[longest] + shift) % drawn.shape[longest]
        spots.append(tuple(where))
    return drawn.at[spots[0]].set(smallest).at[spots[1]].set(high)


def steps_of(rng, dims, cuts, least, high):
    loudness, own = 1.0, jax.random.fold_in(rng, 6)
    for axis_at, shards_of in cuts:
        steps = jnp.exp(jax.random.uniform(jax.random.fold_in(own, axis_at), (shards_of,), jnp.float32, least / len(cuts), high / len(cuts)))
        loudness = loudness * jnp.repeat(steps, dims[axis_at] // shards_of).reshape([-1 if axis == axis_at else 1 for axis in range(len(dims))])
    return loudness


def deal_out(rng, own, number, rows, number_of, top, reach, lean):
    sequence = jax.random.permutation(rng, number_of)
    heavy_load, ordinary = load_shares(number_of, rows * top, reach, lean, True), load_shares(number_of, rows * top, reach, lean, False)
    places = jnp.arange(number_of)

    def named(lengths, offset_by):
        used = int((lengths > 0).sum())
        fixed = max(1, used // 4)
        moved = fixed + (places - fixed + offset_by * (used - fixed)) % max(1, number_of - fixed)
        return jnp.zeros((number_of,), jnp.int32).at[sequence[jnp.where(places < fixed, places, moved)]].set(jnp.asarray(lengths, jnp.int32))

    lengths = jnp.where(number % 4 == 0, named(heavy_load, number // 4), named(ordinary, number - number // 4 - 1))
    mixed = jax.random.permutation(jax.random.fold_in(own, 3), number_of)
    source_of, taker = mixed[0:number_of // 2 * 2:2], mixed[1:number_of // 2 * 2:2]
    room = jnp.minimum(lengths[source_of] - 1, reach - lengths[taker]) // 2
    room = jnp.where((source_of == sequence[0]) | (taker == sequence[0]) | (lengths[taker] == 0), 0, jnp.maximum(room, 0))
    moved = jax.random.randint(jax.random.fold_in(own, 4), (number_of // 2,), 0, 1 << 20) % (room + 1)
    lengths = lengths.at[source_of].add(-moved).at[taker].add(moved)
    labels = jnp.searchsorted(jnp.cumsum(lengths), jnp.arange(rows * top), side="right").astype(jnp.int32)
    table = labels.reshape(top, rows).T
    table = table[jax.random.permutation(jax.random.fold_in(own, 1), rows)]
    offset_by = jax.random.randint(jax.random.fold_in(own, 2), (rows, 1), 0, top)
    return jnp.take_along_axis(table, (jnp.arange(top)[None, :] + offset_by) % top, axis=1)


def load_shares(number_of, total, bound, lean, full):
    portions = [(1 << 20) // math.isqrt(rank ** lean) + 1 for rank in range(1, number_of + 1)]
    largest = bound if full else min(bound, max(-(-total // number_of), total * portions[0] // sum(portions)))
    least = 1 if total - largest >= number_of - 1 else 0
    holding, spare = [largest] + [least] * (number_of - 1), total - largest - least * (number_of - 1)
    while spare > 0:
        movable = [i for i in range(1, number_of) if holding[i] < largest] or [i for i in range(1, number_of) if holding[i] < bound]
        pool, remaining = sum([portions[i] for i in movable]), spare
        for i in movable:
            more = min(bound - holding[i], max(1, remaining * portions[i] // pool), spare)
            holding[i] = holding[i] + more
            spare = spare - more
    return np.array(holding)


def scatter_about(rng, dims, deviation, bound, cuts=(), kind=jnp.bfloat16):
    drawn = deviation * jax.random.normal(rng, dims, jnp.float32)
    if cuts:
        drawn = drawn * steps_of(rng, dims, cuts, -0.22, 0.18)
    return jnp.clip(drawn, -bound, bound).astype(kind)


def setup_inputs(seed: int = 0) -> dict:
    seeds = jax.random.split(jax.random.key(seed), 12)
    hidden_in = scatter_about(seeds[0], (TOKENS, D), 1.0, 6.0, ((0, 64),))
    norm_gain = jnp.clip(1.0 + 0.1 * jax.random.normal(seeds[1], (D,), jnp.float32), 0.5, 1.5)
    expert_ids_keys = jax.random.split(jax.random.fold_in(seeds[2], 1), TOKENS // TOK_REP)
    expert_ids_turns = jax.random.permutation(jax.random.fold_in(seeds[2], 3), TOKENS // TOK_REP)
    expert_ids = jax.vmap(lambda own, number: deal_out(jax.random.fold_in(seeds[2], 2), own, number, TOK_REP, EXPERTS, TOP, CAP, 2))(expert_ids_keys, expert_ids_turns).reshape((TOKENS, TOP))
    gate_scores = touch_ends(jax.random.randint(seeds[3], (TOKENS, TOP), 1, 65), jax.random.fold_in(seeds[3], 1), 1, 64).astype(jnp.int32)
    w_gate = scatter_about(seeds[4], (EXPERTS, FF, D), D ** -0.5, 0.09375, ((0, 64), (1, 16)))
    w_up = scatter_about(seeds[5], (EXPERTS, FF, D), D ** -0.5, 0.09375, ((0, 64), (1, 16)))
    w_down = scatter_about(seeds[6], (EXPERTS, FF, D), FF ** -0.5, 0.1875, ((0, 64), (1, 16)))
    shared_gate = scatter_about(seeds[7], (FF, D), D ** -0.5, 0.09375, ((0, 16),))
    shared_up = scatter_about(seeds[8], (FF, D), D ** -0.5, 0.09375, ((0, 16),))
    shared_down = scatter_about(seeds[9], (FF, D), FF ** -0.5, 0.1875, ((0, 16),))
    out_grad = scatter_about(seeds[10], (TOKENS, D), 1.0, 6.0, ((0, 64),))
    return dict(hidden_in=hidden_in, norm_gain=norm_gain, expert_ids=expert_ids, gate_scores=gate_scores, w_gate=w_gate, w_up=w_up, w_down=w_down, shared_gate=shared_gate, shared_up=shared_up, shared_down=shared_down, out_grad=out_grad)


def silu_slope(values):
    sigmoid_v = jax.nn.sigmoid(values)
    return sigmoid_v * (1.0 + values * (1.0 - sigmoid_v))

def round_kept(values):
    narrow = lax.optimization_barrier(values.astype(jnp.bfloat16))
    return narrow.astype(jnp.float32)

def expert_pass(operands):
    rows_in, cot_rows, gate_mat, up_mat, down_mat = operands
    row_count, model_width = rows_in.shape
    unit_count = gate_mat.shape[0] // N_EXPERT
    pre_gate = jnp.dot(rows_in, gate_mat.T, preferred_element_type=jnp.float32)
    pre_up = jnp.dot(rows_in, up_mat.T, preferred_element_type=jnp.float32)
    activation = (jax.nn.silu(pre_gate) * pre_up).astype(jnp.bfloat16)
    act_blocks = activation.astype(jnp.float32).reshape(row_count, N_EXPERT, unit_count)
    down_blocks = down_mat.astype(jnp.float32).reshape(N_EXPERT, unit_count, model_width)
    partials = jnp.einsum('rbu,bud->rbd', act_blocks, down_blocks)
    expert_out = lax.optimization_barrier(jnp.sum(round_kept(partials), axis=1))
    act_grad = jnp.dot(cot_rows, down_mat.T, preferred_element_type=jnp.float32)
    gate_delta = (act_grad * pre_up * silu_slope(pre_gate)).astype(jnp.bfloat16)
    up_delta = (act_grad * jax.nn.silu(pre_gate)).astype(jnp.bfloat16)
    gate_blocks = gate_delta.astype(jnp.float32).reshape(row_count, N_EXPERT, unit_count)
    up_blocks = up_delta.astype(jnp.float32).reshape(row_count, N_EXPERT, unit_count)
    wg_blocks = gate_mat.astype(jnp.float32).reshape(N_EXPERT, unit_count, model_width)
    wu_blocks = up_mat.astype(jnp.float32).reshape(N_EXPERT, unit_count, model_width)
    in_partials = jnp.einsum('rbu,bud->rbd', gate_blocks, wg_blocks) + jnp.einsum('rbu,bud->rbd', up_blocks, wu_blocks)
    expert_in = lax.optimization_barrier(jnp.sum(round_kept(in_partials), axis=1))
    gate_grad = jnp.dot(gate_delta.T, rows_in, preferred_element_type=jnp.float32).astype(jnp.bfloat16)
    up_grad = jnp.dot(up_delta.T, rows_in, preferred_element_type=jnp.float32).astype(jnp.bfloat16)
    down_grad = jnp.dot(activation.T, cot_rows, preferred_element_type=jnp.float32).astype(jnp.bfloat16)
    return (expert_out, expert_in, gate_grad, up_grad, down_grad)

def reference(hidden_in, norm_gain, expert_ids, gate_scores, w_gate, w_up, w_down, shared_gate, shared_up, shared_down, out_grad):
    widened = hidden_in.astype(jnp.float32)
    inv_rms = lax.rsqrt(lax.optimization_barrier(jnp.mean(widened * widened, axis=-1, keepdims=True)) + 1e-06)
    normalized = widened * inv_rms
    normed = (normalized * norm_gain).astype(jnp.bfloat16)
    scores = gate_scores.astype(jnp.float32)
    gate_weights = 2.5 * scores / lax.optimization_barrier(jnp.sum(scores, axis=-1, keepdims=True))
    pair_ids = expert_ids.reshape(N_REPLICA, TOK_REP * TOP)
    expert_range = jnp.arange(EXPERTS, dtype=jnp.int32)
    onehot = (pair_ids[:, :, None] == expert_range[None, None, :]).astype(jnp.int32)
    earlier = jnp.cumsum(onehot, axis=1) - onehot
    ranking = lax.optimization_barrier(jnp.sum(earlier * onehot, axis=2))
    source = jnp.arange(N_REPLICA, dtype=jnp.int32)[:, None]
    slot_index = ((pair_ids * N_REPLICA + source) * CAP + ranking).reshape(-1).astype(jnp.int32)
    scaled_grad = (gate_weights[:, :, None] * out_grad.astype(jnp.float32)[:, None, :]).astype(jnp.bfloat16).reshape(-1, D)
    repeated = jnp.repeat(normed, TOP, axis=0)
    slot_total = EXPERTS * N_REPLICA * CAP
    row_buffer = jnp.zeros((slot_total, D), jnp.bfloat16).at[slot_index].set(repeated)
    cot_buffer = jnp.zeros((slot_total, D), jnp.bfloat16).at[slot_index].set(scaled_grad)
    row_buffer = row_buffer.reshape(EXPERTS, N_REPLICA * CAP, D)
    cot_buffer = cot_buffer.reshape(EXPERTS, N_REPLICA * CAP, D)
    out_buffer, in_buffer, gate_grad, up_grad, down_grad = lax.map(expert_pass, (row_buffer, cot_buffer, w_gate, w_up, w_down))
    out_pairs = out_buffer.reshape(slot_total, D)[slot_index].reshape(TOKENS, TOP, D)
    in_pairs = in_buffer.reshape(slot_total, D)[slot_index].reshape(TOKENS, TOP, D)
    shared_pre_gate = jnp.dot(normed, shared_gate.T, preferred_element_type=jnp.float32)
    shared_pre_up = jnp.dot(normed, shared_up.T, preferred_element_type=jnp.float32)
    shared_act = (jax.nn.silu(shared_pre_gate) * shared_pre_up).astype(jnp.bfloat16)
    shared_out = jnp.dot(shared_act, shared_down, preferred_element_type=jnp.float32)
    shared_act_grad = jnp.dot(out_grad, shared_down.T, preferred_element_type=jnp.float32)
    shared_gate_delta = (shared_act_grad * shared_pre_up * silu_slope(shared_pre_gate)).astype(jnp.bfloat16)
    shared_up_delta = (shared_act_grad * jax.nn.silu(shared_pre_gate)).astype(jnp.bfloat16)
    shared_in = jnp.dot(shared_gate_delta, shared_gate, preferred_element_type=jnp.float32) + jnp.dot(shared_up_delta, shared_up, preferred_element_type=jnp.float32)
    moe_out = (lax.optimization_barrier(jnp.sum(gate_weights[:, :, None] * out_pairs, axis=1)) + shared_out).astype(jnp.bfloat16)
    normed_grad = lax.optimization_barrier(jnp.sum(in_pairs, axis=1)) + shared_in
    gain_grad = lax.optimization_barrier(jnp.sum(normed_grad * normalized, axis=0))
    scaled = normed_grad * norm_gain
    hidden_grad = (inv_rms * (scaled - normalized * lax.optimization_barrier(jnp.mean(scaled * normalized, axis=-1, keepdims=True)))).astype(jnp.bfloat16)
    shared_gate_grad = jnp.dot(shared_gate_delta.T, normed, preferred_element_type=jnp.float32).astype(jnp.bfloat16)
    shared_up_grad = jnp.dot(shared_up_delta.T, normed, preferred_element_type=jnp.float32).astype(jnp.bfloat16)
    shared_down_grad = jnp.dot(shared_act.T, out_grad, preferred_element_type=jnp.float32).astype(jnp.bfloat16)
    return (moe_out, hidden_grad, gain_grad, gate_grad, up_grad, down_grad, shared_gate_grad, shared_up_grad, shared_down_grad)
```

```python
import jax
import jax.numpy as jnp
from jax import lax
from jax.experimental import pallas as pl
from jax.experimental.pallas import tpu as pltpu
from jax.sharding import PartitionSpec as P

F32, BF16 = jnp.float32, jnp.bfloat16
MESH = pl.DeviceIdType.MESH
LANE = 128
WIDTH, UNITS, TOK, FAN = 3584, 64, 16, 8
RING, PEERS, SLOTS = 8, 64, 4
QUARTER = WIDTH // 4
TILES = QUARTER // LANE
HALF_ROWS = PEERS * SLOTS // 2
UNIT_ROWS = HALF_ROWS + TOK
SPLIT = 64
COLS = WIDTH // PEERS
PACK = 384


def iota(shape, axis):
    return lax.broadcasted_iota(jnp.int32, shape, axis)


def mul(left, right):
    return jnp.dot(left, right, preferred_element_type=F32)


def mul_nt(left, right):
    return lax.dot_general(left, right, (((1,), (1,)), ((), ())), preferred_element_type=F32)


def mul_tn(left, right):
    return lax.dot_general(left, right, (((0,), (0,)), ((), ())), preferred_element_type=F32)


def silu_slope(values, sig):
    return sig * (1.0 + values * (1.0 - sig))


def sigmoid(values):
    return 1.0 / (1.0 + jnp.exp(-values))


def feature_tile(f, j):
    return slice(f * QUARTER + j * LANE, f * QUARTER + (j + 1) * LANE)


def features(f):
    return slice(f * QUARTER, (f + 1) * QUARTER)


def layer_kernel(
    ids_ref, scores_ref, hidden_ref, gain_ref, grad_ref,
    wg_hbm, wu_hbm, wd_hbm, sg_hbm, su_hbm, sd_hbm,
    moe_ref, hidden_grad_ref, gain_grad_ref, gg_ref, ug_ref, dg_ref, shared_ref,
    wg, wu, wd, sg, su, sd, load_sem,
    normed_ref, normalized_ref,
    place_hi_ref, place_lo_ref,
    send1, recv1, units, parts, sibs,
    ring_up, ring_dn, got_up, got_dn, final_ref,
    side_send, side_recv, send2, recv2,
    tok_ref, tok_sib, full_ref, gain_send, gain_recv,
    s1_s, s1_r, side_s, side_r, s2_s, s2_r, g_s, g_r,
    up_s, up_r, dn_s, dn_r, hand_s, hand_r, sib_s, sib_r,
    rup_s, rup_r, rdn_s, rdn_r, t_s, t_r, e_s, e_r,
):
    expert = lax.axis_index("expert")
    me = lax.axis_index("replica")
    y, core = expert // 2, expert % 2
    quarter = y % 4
    is_rows = y < 4
    sibling = expert + 1 - 2 * core
    up = ((y + 1) % RING) * 2 + core
    down = ((y + RING - 1) % RING) * 2 + core

    def at_replica(peer):
        return (expert, peer)

    def at_expert(other):
        return (other, me)

    def remote(src, dst, send, recv, device):
        return pltpu.make_async_remote_copy(
            src_ref=src, dst_ref=dst, send_sem=send, recv_sem=recv, device_id=device, device_id_type=MESH
        )

    barrier = pltpu.get_barrier_semaphore()

    def greet_replica(k, carry):
        pl.semaphore_signal(barrier, inc=1, device_id=at_replica((me + k) % PEERS), device_id_type=MESH)
        return carry

    def greet_chip(k, carry):
        pl.semaphore_signal(
            barrier, inc=1, device_id=at_expert(((y + k) % RING) * 2 + core), device_id_type=MESH
        )
        return carry

    lax.fori_loop(1, PEERS, greet_replica, 0)
    lax.fori_loop(1, RING, greet_chip, 0)
    pl.semaphore_signal(barrier, inc=1, device_id=at_expert(sibling), device_id_type=MESH)

    loads = []
    for n, (src, dst) in enumerate(((sg_hbm, sg), (su_hbm, su), (sd_hbm, sd), (wg_hbm, wg), (wu_hbm, wu), (wd_hbm, wd))):
        loads.append(pltpu.make_async_copy(src, dst, load_sem.at[n]))
        loads[-1].start()

    widened = hidden_ref[...].astype(F32)
    inv_rms = lax.rsqrt(jnp.mean(widened * widened, axis=-1, keepdims=True) + 1e-06)
    normalized = widened * inv_rms
    normalized_ref[...] = normalized
    normed_ref[...] = (normalized * gain_ref[...]).astype(BF16)

    scores = scores_ref[...]
    weights = 2.5 * scores / jnp.sum(scores, axis=0, keepdims=True)
    expert_row = iota((PEERS, TOK), 0)
    member = jnp.zeros((PEERS, TOK), F32)
    gate = jnp.zeros((PEERS, TOK), F32)
    for k in range(FAN):
        hit = expert_row == ids_ref[k : k + 1, :]
        member = member + jnp.where(hit, 1.0, 0.0)
        gate = gate + jnp.where(hit, weights[k : k + 1, :], 0.0)
    before = jnp.where(iota((TOK, TOK), 0) < iota((TOK, TOK), 1), 1.0, 0.0).astype(BF16)
    rank = mul(member.astype(BF16), before)
    code = jnp.where(member > 0.5, rank, -1.0).astype(BF16)
    gate_hi = gate.astype(BF16)
    gate_lo = (gate - gate_hi.astype(F32)).astype(BF16)

    wide = TILES * TOK
    rows = PEERS * 16
    spread = jnp.where(iota((rows, PEERS), 0) // 16 == iota((rows, PEERS), 1), 1.0, 0.0).astype(BF16)
    tile = jnp.where(iota((TOK, wide), 1) % TOK == iota((TOK, wide), 0), 1.0, 0.0).astype(BF16)

    def expand(small):
        return mul(spread, mul(small, tile).astype(BF16))

    row_at, col_at = iota((rows, wide), 0), iota((rows, wide), 1)
    slot_of = (2 * core + row_at % 2).astype(F32)
    chosen = (expand(code) == slot_of) & ((row_at % 16) // 2 == col_at // TOK)
    onehot = jnp.where(chosen, 1.0, 0.0)
    hi_full = onehot * expand(gate_hi)
    lo_full = onehot * expand(gate_lo)
    place = onehot.astype(BF16)
    place_hi_ref[...] = jnp.where(is_rows, hi_full, onehot).astype(BF16)
    place_lo_ref[...] = jnp.where(is_rows, lo_full, 0.0).astype(BF16)
    row_scale = jnp.where(is_rows, 1.0, jnp.sum(hi_full + lo_full, axis=1, keepdims=True))

    mine = pl.ds(pl.multiple_of(quarter * QUARTER, LANE), QUARTER)
    source = jnp.where(is_rows, normed_ref[:, mine], grad_ref[:, mine])
    stacked = jnp.concatenate([source[:, j * LANE : (j + 1) * LANE] for j in range(TILES)], axis=0)
    outgoing = (mul(place, stacked) * row_scale).astype(BF16)
    send1[...] = outgoing.reshape(PEERS, 16, LANE)
    recv1[pl.ds(me, 1)] = send1[pl.ds(me, 1)]

    pl.semaphore_wait(barrier, PEERS - 1 + RING - 1 + 1)

    def exchange(src, dst, sends, recvs):
        def start(k, carry):
            peer = (me + k) % PEERS
            remote(src.at[peer], dst.at[me], sends.at[peer], recvs.at[me], at_replica(peer)).start()
            return carry

        lax.fori_loop(1, PEERS, start, 0)

    def arrived(dst, recvs, sends):
        def wait(k, carry):
            peer = (me + k) % PEERS
            remote(dst.at[peer], dst.at[peer], sends.at[peer], recvs.at[peer], at_replica(peer)).wait_recv()
            return carry

        lax.fori_loop(1, PEERS, wait, 0)

    def sent(src, sends, recvs):
        def wait(k, carry):
            peer = (me + k) % PEERS
            remote(src.at[peer], src.at[peer], sends.at[peer], recvs.at[peer], at_replica(peer)).wait_send()
            return carry

        lax.fori_loop(1, PEERS, wait, 0)

    exchange(send1, recv1, s1_s, s1_r)

    for load in loads[:3]:
        load.wait()
    normed = normed_ref[...]
    shared_pre = mul_nt(normed, sg[...])
    shared_up = mul_nt(normed, su[...])
    shared_sig = sigmoid(shared_pre)
    shared_silu = shared_pre * shared_sig
    shared_act = (shared_silu * shared_up).astype(BF16)
    shared_act_grad = mul_nt(grad_ref[...], sd[...])
    shared_gate_delta = (shared_act_grad * shared_up * silu_slope(shared_pre, shared_sig)).astype(BF16)
    shared_up_delta = (shared_act_grad * shared_silu).astype(BF16)
    for f in range(4):
        parts[f, 0, HALF_ROWS:, :] = mul(shared_act, sd[:, features(f)]).astype(BF16)
        parts[4 + f, 0, HALF_ROWS:, :] = (
            mul(shared_gate_delta, sg[:, features(f)]) + mul(shared_up_delta, su[:, features(f)])
        ).astype(BF16)
        parts[f, 1, HALF_ROWS:, :] = jnp.zeros((TOK, QUARTER), BF16)
        parts[4 + f, 1, HALF_ROWS:, :] = jnp.zeros((TOK, QUARTER), BF16)

    deltas = jnp.concatenate(
        [shared_gate_delta, shared_up_delta, shared_act, jnp.zeros((TOK, UNITS), BF16)], axis=1
    )
    side_send[:, :, LANE:] = jnp.broadcast_to(deltas[None], (PEERS, TOK, 2 * LANE))
    for m in range(16):
        first = min(m * COLS // LANE, TILES - 2)
        offset = m * COLS - first * LANE
        window = slice(first * LANE, (first + 2) * LANE)
        both = jnp.concatenate(
            [
                jnp.concatenate([ref[:, features(f)][:, window] for f in range(4)], axis=0)
                for ref in (normed_ref, grad_ref)
            ],
            axis=1,
        )
        at, lane = iota((4 * LANE, LANE), 0), iota((4 * LANE, LANE), 1)
        from_row = (at < 2 * LANE) & (at - offset == lane) & (lane < COLS)
        from_grad = (at >= 2 * LANE) & (at - 2 * LANE - offset == lane - COLS) & (lane >= COLS) & (lane < 2 * COLS)
        moved = mul(both, jnp.where(from_row | from_grad, 1.0, 0.0).astype(BF16)).astype(BF16)
        for f in range(4):
            side_send[16 * f + m, :, :LANE] = moved[f * TOK : (f + 1) * TOK]
    side_recv[pl.ds(me, 1)] = side_send[pl.ds(me, 1)]

    def unit_to_message(shape, unit_axis):
        at = iota(shape, unit_axis)
        lane = at % LANE
        message = (lane // 2) * 16 + (at // LANE) * 2 + lane % 2
        return jnp.where(message == iota(shape, 1 - unit_axis), 1.0, 0.0).astype(BF16)

    pick = unit_to_message((TILES * HALF_ROWS, rows), 0)
    arrived(recv1, s1_r, s1_s)
    gathered = mul(pick, recv1[...].reshape(rows, LANE)).astype(BF16)
    for j in range(TILES):
        units[y, core, :, j * LANE : (j + 1) * LANE] = gathered[j * HALF_ROWS : (j + 1) * HALF_ROWS]

    exchange(side_send, side_recv, side_s, side_r)

    def unit(chip, lo=0, hi=HALF_ROWS):
        return units.at[chip, core, lo:hi]

    def ring_copy(step, way):
        chip = (y + RING - step) % RING if way == 0 else (y + step) % RING
        lo, hi = (0, HALF_ROWS) if step < 3 else ((0, SPLIT) if way == 0 else (SPLIT, HALF_ROWS))
        sends, recvs, device = ((up_s, up_r, up), (dn_s, dn_r, down))[way]
        ref = unit(chip, lo, hi)
        return remote(ref, ref, sends.at[step], recvs.at[step], at_expert(device))

    def ring_arrival(step, way):
        chip = (y + RING - 1 - step) % RING if way == 0 else (y + 1 + step) % RING
        lo, hi = (0, HALF_ROWS) if step < 3 else ((0, SPLIT) if way == 0 else (SPLIT, HALF_ROWS))
        sends, recvs, device = ((up_s, up_r, up), (dn_s, dn_r, down))[way]
        ref = unit(chip, lo, hi)
        return ref, remote(ref, ref, sends.at[step], recvs.at[step], at_expert(device))

    def hand_over(n, ref):
        return remote(ref, ref, hand_s.at[n], hand_r.at[n], at_expert(sibling))

    def hand_arrival(n, chip, lo, hi):
        ref = units.at[chip, 1 - core, lo:hi]
        return remote(ref, ref, hand_s.at[n], hand_r.at[n], at_expert(sibling))

    waits = []
    for way in (0, 1):
        copy = ring_copy(0, way)
        copy.start()
        waits.append(copy)
    copy = hand_over(0, unit(y))
    copy.start()
    waits.append(copy)
    hands = [hand_arrival(0, y, 0, HALF_ROWS)]
    for step in range(4):
        for way in (0, 1):
            ref, arrival = ring_arrival(step, way)
            arrival.wait_recv()
            if step < 3:
                copy = ring_copy(step + 1, way)
                copy.start()
                waits.append(copy)
            number = 1 + 2 * step + way
            copy = hand_over(number, ref)
            copy.start()
            waits.append(copy)
            chip = (y + RING - 1 - step) % RING if way == 0 else (y + 1 + step) % RING
            lo, hi = (0, HALF_ROWS) if step < 3 else ((0, SPLIT) if way == 0 else (SPLIT, HALF_ROWS))
            hands.append(hand_arrival(number, chip, lo, hi))
    for load in loads[3:]:
        load.wait()
    for hand in hands:
        hand.wait_recv()

    def unit_rows(chip):
        return units[chip].reshape(2 * HALF_ROWS, QUARTER)

    pre_gate = sum(mul_nt(unit_rows(f), wg[:, features(f)]) for f in range(4))
    pre_up = sum(mul_nt(unit_rows(f), wu[:, features(f)]) for f in range(4))
    act_grad = sum(mul_nt(unit_rows(4 + f), wd[:, features(f)]) for f in range(4))
    sig = sigmoid(pre_gate)
    silu = pre_gate * sig
    activation = (silu * pre_up).astype(BF16)
    gate_delta = (act_grad * pre_up * silu_slope(pre_gate, sig)).astype(BF16)
    up_delta = (act_grad * silu).astype(BF16)
    for f in range(4):
        out_part = mul(activation, wd[:, features(f)]).astype(BF16)
        parts[f, :, :HALF_ROWS, :] = out_part.reshape(2, HALF_ROWS, QUARTER)
        in_part = (mul(gate_delta, wg[:, features(f)]) + mul(up_delta, wu[:, features(f)])).astype(BF16)
        parts[4 + f, :, :HALF_ROWS, :] = in_part.reshape(2, HALF_ROWS, QUARTER)

    order = (4, 3, 5, 2, 6, 1, 7, 0)
    for n, off in enumerate(order):
        chip = (y + off) % RING
        copy = remote(
            parts.at[chip, 1 - core], sibs.at[chip], sib_s.at[n], sib_r.at[n], at_expert(sibling)
        )
        copy.start()
        waits.append(copy)

    def pair_sum(off):
        chip = (y + off) % RING
        n = order.index(off)
        remote(sibs.at[chip], sibs.at[chip], sib_s.at[n], sib_r.at[n], at_expert(sibling)).wait_recv()
        return parts[chip, core].astype(F32) + sibs[chip].astype(F32)

    far = pair_sum(4).astype(BF16)
    ring_up[0, :SPLIT] = far[:SPLIT]
    ring_dn[0, SPLIT:] = far[SPLIT:]

    def reduce_copy(step, way):
        lo, hi = (0, UNIT_ROWS) if step else ((0, SPLIT) if way == 0 else (SPLIT, UNIT_ROWS))
        src, dst = ((ring_up, got_up), (ring_dn, got_dn))[way]
        sends, recvs, device = ((rup_s, rup_r, up), (rdn_s, rdn_r, down))[way]
        return remote(
            src.at[step, lo:hi], dst.at[step, lo:hi], sends.at[step], recvs.at[step], at_expert(device)
        )

    for way in (0, 1):
        copy = reduce_copy(0, way)
        copy.start()
        waits.append(copy)
    for step in range(1, 4):
        for way in (0, 1):
            total = pair_sum(4 - step if way == 0 else 4 + step)
            mine_ref, got = ((ring_up, got_up), (ring_dn, got_dn))[way]
            reduce_copy(step - 1, way).wait_recv()
            if step > 1:
                mine_ref[step] = (total + got[step - 1].astype(F32)).astype(BF16)
            elif way == 0:
                mine_ref[step, :SPLIT] = (total[:SPLIT] + got[0, :SPLIT].astype(F32)).astype(BF16)
                mine_ref[step, SPLIT:] = total[SPLIT:].astype(BF16)
            else:
                mine_ref[step, :SPLIT] = total[:SPLIT].astype(BF16)
                mine_ref[step, SPLIT:] = (total[SPLIT:] + got[0, SPLIT:].astype(F32)).astype(BF16)
            copy = reduce_copy(step, way)
            copy.start()
            waits.append(copy)
    for f in range(4):
        row_block, cot_block = unit_rows(f), unit_rows(4 + f)
        gg_ref[:, features(f)] = mul_tn(gate_delta, row_block).astype(BF16)
        ug_ref[:, features(f)] = mul_tn(up_delta, row_block).astype(BF16)
        dg_ref[:, features(f)] = mul_tn(activation, cot_block).astype(BF16)
    own = pair_sum(0)
    for way in (0, 1):
        reduce_copy(3, way).wait_recv()
    final_ref[...] = own + got_up[3].astype(F32) + got_dn[3].astype(F32)

    finished = jnp.concatenate(
        [final_ref[:HALF_ROWS, j * LANE : (j + 1) * LANE].astype(BF16) for j in range(TILES)], axis=0
    )
    spill = unit_to_message((rows, TILES * HALF_ROWS), 1)
    send2[...] = mul(spill, finished).astype(BF16).reshape(PEERS, 16, LANE)
    recv2[pl.ds(me, 1)] = send2[pl.ds(me, 1)]
    exchange(send2, recv2, s2_s, s2_r)

    arrived(side_recv, side_r, side_s)
    every = side_recv[...].reshape(PEERS * TOK, PACK)
    shared_ref[...] = mul_tn(every[:, LANE:], every[:, :LANE]).astype(BF16)

    arrived(recv2, s2_r, s2_s)
    returned = recv2[...].reshape(rows, LANE)
    tokens = mul_tn(place_hi_ref[...], returned) + mul_tn(place_lo_ref[...], returned)
    shared_rows = jnp.concatenate(
        [final_ref[HALF_ROWS:, j * LANE : (j + 1) * LANE] for j in range(TILES)], axis=0
    )
    tok_ref[...] = tokens + shared_rows
    copy = remote(tok_ref, tok_sib, t_s, t_r, at_expert(sibling))
    copy.start()
    waits.append(copy)
    copy.wait_recv()
    full_ref[y] = (tok_ref[...] + tok_sib[...]).astype(BF16)

    def send_full(k, carry):
        chip = (y + k) % RING
        remote(full_ref.at[y], full_ref.at[y], e_s.at[k], e_r.at[k], at_expert(chip * 2 + core)).start()
        return carry

    def wait_full(k, carry):
        chip = (y + RING - k) % RING
        remote(full_ref.at[chip], full_ref.at[chip], e_s.at[k], e_r.at[k], at_expert(chip * 2 + core)).wait_recv()
        return carry

    def wait_full_sent(k, carry):
        remote(full_ref.at[y], full_ref.at[y], e_s.at[k], e_r.at[k], at_expert(up)).wait_send()
        return carry

    lax.fori_loop(1, RING, send_full, 0)
    lax.fori_loop(1, RING, wait_full, 0)

    def grad_tile(f, j):
        return full_ref[4 + f, j * TOK : (j + 1) * TOK, :].astype(F32)

    inner = jnp.zeros((TOK, 1), F32)
    for f in range(4):
        terms = []
        for j in range(TILES):
            at = feature_tile(f, j)
            term = grad_tile(f, j) * normalized_ref[:, at]
            terms.append(jnp.sum(term, axis=0, keepdims=True))
            inner = inner + jnp.sum(term * gain_ref[:, at], axis=1, keepdims=True)
        terms.append(jnp.zeros((1, LANE), F32))
        line = jnp.concatenate(terms, axis=1)
        for m in range(16):
            gain_send[16 * f + m] = line[:, m * COLS : m * COLS + LANE]
    gain_recv[pl.ds(me, 1)] = gain_send[pl.ds(me, 1)]
    exchange(gain_send, gain_recv, g_s, g_r)
    inner = inner * (1.0 / WIDTH)
    inv_again = lax.rsqrt(
        jnp.mean(jnp.square(hidden_ref[...].astype(F32)), axis=-1, keepdims=True) + 1e-06
    )
    for f in range(4):
        for j in range(TILES):
            at = feature_tile(f, j)
            moe_ref[:, at] = full_ref[f, j * TOK : (j + 1) * TOK, :]
            scaled = grad_tile(f, j) * gain_ref[:, at]
            hidden_grad_ref[:, at] = (inv_again * (scaled - normalized_ref[:, at] * inner)).astype(BF16)

    for copy in waits:
        copy.wait_send()
    lax.fori_loop(1, RING, wait_full_sent, 0)
    sent(send1, s1_s, s1_r)
    sent(side_send, side_s, side_r)
    sent(send2, s2_s, s2_r)
    sent(gain_send, g_s, g_r)
    arrived(gain_recv, g_r, g_s)
    gain_grad_ref[...] = jnp.sum(gain_recv[...], axis=0)


def per_device(
    hidden_in, norm_gain, expert_ids, gate_scores, w_gate, w_up, w_down, shared_gate, shared_up, shared_down, out_grad
):
    vmem, hbm = pl.BlockSpec(memory_space=pltpu.VMEM), pl.BlockSpec(memory_space=pl.ANY)
    dma = pltpu.SemaphoreType.DMA
    matrix = (UNITS, WIDTH)
    message = (PEERS, 16, LANE)
    outs = pl.pallas_call(
        layer_kernel,
        out_shape=(
            jax.ShapeDtypeStruct((TOK, WIDTH), BF16),
            jax.ShapeDtypeStruct((TOK, WIDTH), BF16),
            jax.ShapeDtypeStruct((1, LANE), F32),
            jax.ShapeDtypeStruct(matrix, BF16),
            jax.ShapeDtypeStruct(matrix, BF16),
            jax.ShapeDtypeStruct(matrix, BF16),
            jax.ShapeDtypeStruct((2 * LANE, LANE), BF16),
        ),
        in_specs=[vmem] * 5 + [hbm] * 6,
        out_specs=[vmem] * 7,
        scratch_shapes=[pltpu.VMEM(matrix, BF16)] * 6
        + [
            dma((6,)),
            pltpu.VMEM((TOK, WIDTH), BF16),
            pltpu.VMEM((TOK, WIDTH), F32),
            pltpu.VMEM((PEERS * 16, TILES * TOK), BF16),
            pltpu.VMEM((PEERS * 16, TILES * TOK), BF16),
            pltpu.VMEM(message, BF16),
            pltpu.VMEM(message, BF16),
            pltpu.VMEM((RING, 2, HALF_ROWS, QUARTER), BF16),
            pltpu.VMEM((RING, 2, UNIT_ROWS, QUARTER), BF16),
            pltpu.VMEM((RING, UNIT_ROWS, QUARTER), BF16),
        ]
        + [pltpu.VMEM((4, UNIT_ROWS, QUARTER), BF16)] * 4
        + [
            pltpu.VMEM((UNIT_ROWS, QUARTER), F32),
            pltpu.VMEM((PEERS, TOK, PACK), BF16),
            pltpu.VMEM((PEERS, TOK, PACK), BF16),
            pltpu.VMEM(message, BF16),
            pltpu.VMEM(message, BF16),
            pltpu.VMEM((TILES * TOK, LANE), F32),
            pltpu.VMEM((TILES * TOK, LANE), F32),
            pltpu.VMEM((RING, TILES * TOK, LANE), BF16),
            pltpu.VMEM((PEERS, 1, LANE), F32),
            pltpu.VMEM((PEERS, 1, LANE), F32),
        ]
        + [dma((PEERS,))] * 8
        + [dma((4,))] * 4
        + [dma((9,))] * 2
        + [dma((RING,))] * 2
        + [dma((4,))] * 4
        + [dma] * 2
        + [dma((RING,))] * 2,
        compiler_params=pltpu.CompilerParams(
            collective_id=0, has_side_effects=True, vmem_limit_bytes=56 * 1024 * 1024
        ),
    )(
        expert_ids.T,
        gate_scores.astype(F32).T,
        hidden_in,
        norm_gain.reshape(1, WIDTH),
        out_grad,
        w_gate[0],
        w_up[0],
        w_down[0],
        shared_gate,
        shared_up,
        shared_down,
    )
    moe_out, hidden_grad, gain_grad, gate_grad, up_grad, down_grad, shared = outs
    return (
        moe_out,
        hidden_grad,
        gain_grad[0, :COLS],
        gate_grad[None],
        up_grad[None],
        down_grad[None],
        shared[:UNITS, :COLS],
        shared[UNITS : 2 * UNITS, :COLS],
        shared[2 * UNITS : 3 * UNITS, COLS : 2 * COLS],
    )


def solution(mesh):
    rows, weights, shared = P("replica", None), P("replica", "expert", None), P("expert", None)
    return jax.shard_map(
        per_device,
        mesh=mesh,
        in_specs=(rows, P(), rows, rows, weights, weights, weights, shared, shared, shared, rows),
        out_specs=(rows, rows, P("replica"), weights, weights, weights) + (P("expert", "replica"),) * 3,
        check_vma=False,
    )
```

```python
import jax
import jax.numpy as jnp
from jax import lax
from jax.experimental import pallas as pl
from jax.experimental.pallas import tpu as pltpu
from jax.sharding import PartitionSpec as P

F32, BF16 = jnp.float32, jnp.bfloat16
MESH = pl.DeviceIdType.MESH
LANE = 128
WIDTH, UNITS, TOK, FAN = 3584, 64, 16, 8
RING, PEERS, SLOTS = 8, 64, 4
QUARTER = WIDTH // 4
TILES = QUARTER // LANE
HALF_ROWS = PEERS * SLOTS // 2
UNIT_ROWS = HALF_ROWS + TOK
PARTS = 2 * RING
HALF = PEERS // 2
SPAN = HALF_ROWS // 2
OWN = PEERS - 1
COLS = WIDTH // PEERS


def iota(shape, axis):
    return lax.broadcasted_iota(jnp.int32, shape, axis)


def mul(left, right):
    return jnp.dot(left, right, preferred_element_type=F32)


def mul_nt(left, right):
    return lax.dot_general(left, right, (((1,), (1,)), ((), ())), preferred_element_type=F32)


def mul_tn(left, right):
    return lax.dot_general(left, right, (((0,), (0,)), ((), ())), preferred_element_type=F32)


def silu_slope(values, sig):
    return sig * (1.0 + values * (1.0 - sig))


def sigmoid(values):
    return 1.0 / (1.0 + jnp.exp(-values))


def feature_tile(f, j):
    return slice(f * QUARTER + j * LANE, f * QUARTER + (j + 1) * LANE)


def features(f):
    return slice(f * QUARTER, (f + 1) * QUARTER)


def layer_kernel(
    ids_ref, scores_ref, hidden_ref, gain_ref, grad_ref,
    wg_hbm, wu_hbm, wd_hbm, sg_hbm, su_hbm, sd_hbm,
    moe_ref, hidden_grad_ref, gain_grad_ref, shared_gate_ref, shared_up_ref, shared_down_ref,
    gg_hbm, ug_hbm, dg_hbm,
    wg, wu, wd, sg, su, sd, load_sem,
    normed_ref, normalized_ref, back_hi_ref, back_lo_ref, pick_ref, spill_ref,
    send1, recv1, units, parts, sibs,
    ring_up, ring_dn, got_up, got_dn, final_ref,
    side_send, side_recv, side_sib, send2, recv2,
    tok_ref, tok_sib, full_ref, gain_send, gain_recv, gain_all,
    gg_ref, ug_ref, dg_ref, store_sem,
    s1_s, s1_r, side_s, side_r, s2_s, s2_r, g_s, g_r,
    up_s, up_r, dn_s, dn_r, rup_s, rup_r, rdn_s, rdn_r, hand_s, hand_r, sib_s, sib_r,
    e_s, e_r, gb_s, gb_r, pair_s, pair_r,
):
    expert = lax.axis_index("expert")
    me = lax.axis_index("replica")
    y, core = expert // 2, expert % 2
    x, z = me // 16, me % 16
    quarter = y % 4
    is_rows = y < 4
    sibling = expert + 1 - 2 * core

    def at_replica(peer):
        return (expert, peer)

    def at_expert(other):
        return (other, me)

    def remote(src, dst, send, recv, device):
        return pltpu.make_async_remote_copy(
            src_ref=src, dst_ref=dst, send_sem=send, recv_sem=recv, device_id=device, device_id_type=MESH
        )

    def along_z(n):
        t = 15 - n
        odd = t % 2
        return odd * ((t + 1) // 2) + (1 - odd) * (16 - t // 2)

    def along_x(c):
        return (c + 1) % 4

    barrier = pltpu.get_barrier_semaphore()

    def greet_replica(k, carry):
        pl.semaphore_signal(barrier, inc=1, device_id=at_replica((me + k) % PEERS), device_id_type=MESH)
        return carry

    def greet_expert(k, carry):
        pl.semaphore_signal(barrier, inc=1, device_id=at_expert((expert + k) % PARTS), device_id_type=MESH)
        return carry

    lax.fori_loop(1, PEERS, greet_replica, 0)
    lax.fori_loop(1, PARTS, greet_expert, 0)

    loads = []
    for n, (src, dst) in enumerate(
        ((sg_hbm, sg), (su_hbm, su), (sd_hbm, sd), (wg_hbm.at[0], wg), (wu_hbm.at[0], wu), (wd_hbm.at[0], wd))
    ):
        loads.append(pltpu.make_async_copy(src, dst, load_sem.at[n]))
        loads[-1].start()

    widened = hidden_ref[...].astype(F32)
    inv_rms = lax.rsqrt(jnp.mean(widened * widened, axis=-1, keepdims=True) + 1e-06)
    for n in range(4 * TILES):
        at = slice(n * LANE, (n + 1) * LANE)
        normalized = widened[:, at] * inv_rms
        normalized_ref[:, at] = normalized
        normed_ref[:, at] = (normalized * gain_ref[n : n + 1, :]).astype(BF16)

    scores = scores_ref[...].astype(F32)
    weights = 2.5 * scores / jnp.sum(scores, axis=0, keepdims=True)
    row_q = iota((PEERS, TOK), 0)
    expert_of = ((x + along_x(row_q % 4)) % 4) * 16 + (z + along_z(row_q // 4)) % 16
    member = jnp.zeros((PEERS, TOK), F32)
    gate = jnp.zeros((PEERS, TOK), F32)
    for k in range(FAN):
        hit = expert_of == ids_ref[k : k + 1, :]
        member = member + jnp.where(hit, 1.0, 0.0)
        gate = gate + jnp.where(hit, weights[k : k + 1, :], 0.0)
    before = jnp.where(iota((TOK, TOK), 0) < iota((TOK, TOK), 1), 1.0, 0.0).astype(BF16)
    rank = mul(member.astype(BF16), before)
    code = jnp.where(member > 0.5, rank - (2 * core).astype(F32), -32.0).astype(BF16)
    gate_hi = gate.astype(BF16).astype(F32)
    gate_lo = gate - gate_hi

    rows = PEERS * 16
    at_row, at_lane = iota((rows, LANE), 0), iota((rows, LANE), 1)
    belongs = (at_lane == at_row // 16) | (at_lane == PEERS + (at_row % 16) // 2)
    belongs = belongs | ((at_lane == PEERS + 8) & (at_row % 2 == 1))
    spread = jnp.where(belongs, 1.0, 0.0).astype(BF16)
    tile = jnp.where(iota((TOK, LANE), 1) % TOK == iota((TOK, LANE), 0), 1.0, 0.0).astype(BF16)
    low, lane = iota((PEERS, LANE), 0), iota((PEERS, LANE), 1)
    rest = jnp.where(low < 8, jnp.where((low == lane // TOK) & (low < TILES), 0.0, -64.0), 0.0)
    rest = jnp.where(low == 8, -1.0, rest)

    def expand(small, below):
        return mul(spread, jnp.concatenate([mul(small.astype(BF16), tile), below], axis=0).astype(BF16))

    nothing = jnp.zeros((PEERS, LANE), F32)
    widths = [mul(small.astype(BF16), tile) for small in (code, jnp.where(is_rows, member, gate_hi))]
    table = jnp.concatenate(
        [jnp.concatenate(widths, axis=1), jnp.concatenate([rest, nothing], axis=1)], axis=0
    )
    found = mul(spread, table.astype(BF16))
    chosen = found[:, :LANE] == 0.0
    place = jnp.where(chosen, found[:, LANE:], 0.0).astype(BF16)
    mine = pl.ds(pl.multiple_of(quarter * QUARTER, LANE), QUARTER)
    source = jnp.where(is_rows, normed_ref[:, mine], grad_ref[:, mine])
    stacked = jnp.concatenate(
        [source[:, j * LANE : (j + 1) * LANE] for j in range(TILES)] + [jnp.zeros((TOK, LANE), BF16)], axis=0
    )
    send1[...] = mul(place, stacked).astype(BF16).reshape(PEERS, 16, LANE)
    recv1[OWN] = send1[OWN]

    pl.semaphore_wait(barrier, PEERS - 1 + PARTS - 1)

    def exchange(src, dst, send, recv, lo, hi, back=False):
        planes = []
        for c in range(4):
            planes.append(lax.rem(x + (4 - along_x(c) if back else along_x(c)), 4) * 16)

        def some(n, count):
            shift = along_z(n)
            row = lax.rem(z + (16 - shift if back else shift) + 16, 16)
            for c in range(count):
                q = 4 * n + c
                remote(src.at[q], dst.at[q], send, recv, at_replica(planes[c] + row)).start()

        def step(n, carry):
            some(n, 4)
            return carry

        lax.fori_loop(lo // 4, min(hi, OWN) // 4, step, 0)
        if hi > OWN:
            some(OWN // 4, 3)

    def arrived(dst, send, recv, lo, hi):
        ref = dst.at[lo : min(hi, OWN)]
        remote(ref, ref, send, recv, at_replica((me + 1) % PEERS)).wait_recv()

    def sent(src, send, recv):
        ref = src.at[:OWN]
        remote(ref, ref, send, recv, at_replica((me + 1) % PEERS)).wait_send()

    exchange(send1, recv1, s1_s, s1_r.at[0], HALF, PEERS)
    exchange(send1, recv1, s1_s, s1_r.at[1], 0, HALF)

    for load in loads[:3]:
        load.wait()
    normed = normed_ref[...]
    shared_pre = mul_nt(normed, sg[...])
    shared_up = mul_nt(normed, su[...])
    shared_sig = sigmoid(shared_pre)
    shared_silu = shared_pre * shared_sig
    shared_act = (shared_silu * shared_up).astype(BF16)
    shared_act_grad = mul_nt(grad_ref[...], sd[...])
    shared_gate_delta = (shared_act_grad * shared_up * silu_slope(shared_pre, shared_sig)).astype(BF16)
    shared_up_delta = (shared_act_grad * shared_silu).astype(BF16)

    def unit_to_message(shape, unit_axis):
        at = iota(shape, unit_axis)
        row = at % SPAN
        message = (row // 2) * 16 + (at // SPAN) * 2 + row % 2
        return jnp.where(message == iota(shape, 1 - unit_axis), 1.0, 0.0).astype(BF16)

    pick_ref[...] = unit_to_message((TILES * SPAN, HALF * 16), 0)

    def unpack(chunk):
        q = 0 if chunk else HALF
        lo = 0 if chunk else SPAN
        arrived(recv1, s1_s, s1_r.at[chunk], q, q + HALF)
        gathered = mul(pick_ref[...], recv1[q : q + HALF].reshape(HALF * 16, LANE)).astype(BF16)
        for j in range(TILES):
            units[y, core, lo : lo + SPAN, j * LANE : (j + 1) * LANE] = gathered[j * SPAN : (j + 1) * SPAN]

    waits, hands = [], [[], []]

    def launch(copy):
        copy.start()
        waits.append(copy)

    def chip_at(way, distance):
        return (y + distance) % RING if way == 0 else (y + RING - distance) % RING

    def gather_rows(chunk, distance, way):
        lo = 0 if chunk else SPAN
        if distance < 4:
            return lo, lo + SPAN
        return (lo, lo + SPAN // 2) if way == 0 else (lo + SPAN // 2, lo + SPAN)

    def gather_copy(chunk, distance, way, chip, hops=1):
        lo, hi = gather_rows(chunk, distance, way)
        sends, recvs = ((up_s, up_r), (dn_s, dn_r))[way]
        ref = units.at[chip, core, lo:hi]
        n = chunk * 4 + distance - 1
        return remote(ref, ref, sends.at[n], recvs.at[n], at_expert(chip_at(way, hops) * 2 + core))

    def hand_over(chunk, n, chip, lo, hi):
        n = chunk * 9 + n
        ref = units.at[chip, core, lo:hi]
        launch(remote(ref, ref, hand_s.at[n], hand_r.at[n], at_expert(sibling)))
        ref = units.at[chip, 1 - core, lo:hi]
        hands[chunk].append(remote(ref, ref, hand_s.at[n], hand_r.at[n], at_expert(sibling)))

    def gather_begin(chunk):
        for distance in (2, 1):
            for way in (0, 1):
                launch(gather_copy(chunk, distance, way, y, distance))
        hand_over(chunk, 0, y, *gather_rows(chunk, 1, 0))

    def gather_arrival(chunk, distance, way):
        chip = chip_at(1 - way, distance)
        gather_copy(chunk, distance, way, chip).wait_recv()
        return chip

    def gather_middle(chunk):
        homes = []
        for way in (0, 1):
            chip = gather_arrival(chunk, 2, way)
            launch(gather_copy(chunk, 4, way, chip, 2))
            launch(gather_copy(chunk, 3, way, chip, 1))
            homes.append(chip)
        for way in (0, 1):
            hand_over(chunk, 3 + way, homes[way], *gather_rows(chunk, 2, way))
        for way in (0, 1):
            chip = gather_arrival(chunk, 1, way)
            hand_over(chunk, 1 + way, chip, *gather_rows(chunk, 1, way))

    def gather_end(chunk):
        for distance in (3, 4):
            for way in (0, 1):
                chip = gather_arrival(chunk, distance, way)
                hand_over(chunk, 2 * distance - 1 + way, chip, *gather_rows(chunk, distance, way))

    unpack(0)
    gather_begin(0)

    for f in range(4):
        parts[f, 0, HALF_ROWS:, :] = mul(shared_act, sd[:, features(f)]).astype(BF16)
        parts[4 + f, 0, HALF_ROWS:, :] = (
            mul(shared_gate_delta, sg[:, features(f)]) + mul(shared_up_delta, su[:, features(f)])
        ).astype(BF16)
        parts[f, 1, HALF_ROWS:, :] = jnp.zeros((TOK, QUARTER), BF16)
        parts[4 + f, 1, HALF_ROWS:, :] = jnp.zeros((TOK, QUARTER), BF16)


    act_wide = jnp.concatenate([shared_act.astype(F32), jnp.zeros((TOK, LANE - UNITS), F32)], axis=1)
    side_send[:, :, :LANE] = jnp.broadcast_to(
        jnp.concatenate([shared_gate_delta, shared_up_delta], axis=1)[None], (PEERS, TOK, LANE)
    )

    def side_columns(m):
        first = min(m * COLS // LANE, TILES - 2)
        offset = m * COLS - first * LANE
        window = slice(first * LANE, (first + 2) * LANE)
        block = jnp.concatenate(
            [
                jnp.where(core == 0, normed_ref[:, features(f)][:, window], grad_ref[:, features(f)][:, window])
                for f in range(4)
            ],
            axis=0,
        )
        at, to = iota((2 * LANE, LANE), 0), iota((2 * LANE, LANE), 1)
        moves = (at - offset == to - UNITS) & (to >= UNITS) & (to < UNITS + COLS)
        moved = mul(block, jnp.where(moves, 1.0, 0.0).astype(BF16))
        for f in range(4):
            ahead = (m + 16 - z) % 16
            place_z = jnp.where(ahead <= 8, 2 * ahead - jnp.where(ahead > 0, 1, 0), 32 - 2 * ahead)
            q = (15 - place_z) * 4 + (f + 7 - x) % 4
            side_send[q, :, LANE:] = (moved[f * TOK : (f + 1) * TOK] + act_wide).astype(BF16)

    for m in range(16):
        side_columns(m)
    gather_middle(0)
    side_recv[OWN] = side_send[OWN]

    spill_ref[...] = unit_to_message((HALF * 16, TILES * SPAN), 1)
    back_hi = jnp.where(chosen, expand(jnp.where(is_rows, gate_hi, member), nothing), 0.0)
    back_lo = jnp.where(chosen, expand(jnp.where(is_rows, gate_lo, 0.0), nothing), 0.0)
    back_hi_ref[...] = jnp.transpose(back_hi).astype(BF16)
    back_lo_ref[...] = jnp.transpose(back_lo).astype(BF16)

    def send_side(batch):
        exchange(side_send, side_recv, side_s, side_r, 16 * batch, 16 * batch + 16)

    unpack(1)
    gather_begin(1)
    send_side(0)
    gather_end(0)
    send_side(1)
    gather_middle(1)
    send_side(2)

    def unit_rows(chip, chunk):
        lo = 0 if chunk else SPAN
        return units[chip, :, lo : lo + SPAN, :].reshape(2 * SPAN, QUARTER)

    def run_expert(chunk):
        lo = 0 if chunk else SPAN
        for hand in hands[chunk]:
            hand.wait_recv()
        pre_gate = sum(mul_nt(unit_rows(f, chunk), wg[:, features(f)]) for f in range(4))
        pre_up = sum(mul_nt(unit_rows(f, chunk), wu[:, features(f)]) for f in range(4))
        act_grad = sum(mul_nt(unit_rows(4 + f, chunk), wd[:, features(f)]) for f in range(4))
        sig = sigmoid(pre_gate)
        silu = pre_gate * sig
        activation = (silu * pre_up).astype(BF16)
        gate_delta = (act_grad * pre_up * silu_slope(pre_gate, sig)).astype(BF16)
        up_delta = (act_grad * silu).astype(BF16)
        for f in range(4):
            out_part = mul(activation, wd[:, features(f)]).astype(BF16)
            parts[f, :, lo : lo + SPAN, :] = out_part.reshape(2, SPAN, QUARTER)
            in_part = (mul(gate_delta, wg[:, features(f)]) + mul(up_delta, wu[:, features(f)])).astype(BF16)
            parts[4 + f, :, lo : lo + SPAN, :] = in_part.reshape(2, SPAN, QUARTER)
        return activation, gate_delta, up_delta

    order = (4, 3, 5, 1, 7, 2, 6, 0)

    def reduce_rows(chunk):
        lo, hi = (0, SPAN) if chunk else (SPAN, UNIT_ROWS)
        return lo, lo + SPAN // 2, hi

    def pair_copy(chunk, n, chip):
        lo, _, hi = reduce_rows(chunk)
        n = chunk * 8 + n
        return remote(
            parts.at[chip, 1 - core, lo:hi], sibs.at[chip, lo:hi], sib_s.at[n], sib_r.at[n], at_expert(sibling)
        )

    def pair_begin(chunk):
        for n, off in enumerate(order):
            launch(pair_copy(chunk, n, (y + off) % RING))

    def pair_sum(chunk, off):
        lo, _, hi = reduce_rows(chunk)
        chip = (y + off) % RING
        pair_copy(chunk, order.index(off), chip).wait_recv()
        return parts[chip, core, lo:hi].astype(F32) + sibs[chip, lo:hi].astype(F32)

    slot_hops = (2, 1, 1, 2)

    def reduce_copy(chunk, slot, way):
        lo, mid, hi = reduce_rows(chunk)
        if slot == 0:
            lo, hi = (lo, mid) if way == 0 else (mid, hi)
        src, dst = ((ring_up, got_up), (ring_dn, got_dn))[way]
        sends, recvs = ((rup_s, rup_r), (rdn_s, rdn_r))[way]
        n = chunk * 4 + slot
        device = at_expert(chip_at(way, slot_hops[slot]) * 2 + core)
        return remote(src.at[slot, lo:hi], dst.at[slot, lo:hi], sends.at[n], recvs.at[n], device)

    def offset(way, distance):
        return distance if way == 0 else RING - distance

    def reduce_begin(chunk):
        lo, mid, hi = reduce_rows(chunk)
        far = pair_sum(chunk, 4).astype(BF16)
        ring_up[0, lo:mid] = far[: mid - lo]
        ring_dn[0, mid:hi] = far[mid - lo :]
        for way in (0, 1):
            launch(reduce_copy(chunk, 0, way))
        for slot, distance in ((1, 3), (2, 1)):
            for way in (0, 1):
                (ring_up, ring_dn)[way][slot, lo:hi] = pair_sum(chunk, offset(way, distance)).astype(BF16)
                launch(reduce_copy(chunk, slot, way))

    def reduce_middle(chunk):
        lo, mid, hi = reduce_rows(chunk)
        for way in (0, 1):
            total = pair_sum(chunk, offset(way, 2))
            out, got = ((ring_up, got_up), (ring_dn, got_dn))[way]
            reduce_copy(chunk, 1, way).wait_recv()
            total = total + got[1, lo:hi].astype(F32)
            reduce_copy(chunk, 0, way).wait_recv()
            half, rest_of = total[: mid - lo], total[mid - lo :]
            if way == 0:
                half = half + got[0, lo:mid].astype(F32)
            else:
                rest_of = rest_of + got[0, mid:hi].astype(F32)
            out[3, lo:mid] = half.astype(BF16)
            out[3, mid:hi] = rest_of.astype(BF16)
            launch(reduce_copy(chunk, 3, way))

    def reduce_end(chunk):
        lo, mid, hi = reduce_rows(chunk)
        total = pair_sum(chunk, 0)
        for slot in (2, 3):
            for way in (0, 1):
                reduce_copy(chunk, slot, way).wait_recv()
                total = total + (got_up, got_dn)[way][slot, lo:hi].astype(F32)
        final_ref[lo:hi] = total
        finished = jnp.concatenate(
            [final_ref[lo : lo + SPAN, j * LANE : (j + 1) * LANE].astype(BF16) for j in range(TILES)], axis=0
        )
        q = 0 if chunk else HALF
        send2[q : q + HALF] = mul(spill_ref[...], finished).astype(BF16).reshape(HALF, 16, LANE)
        if not chunk:
            recv2[OWN] = send2[OWN]
        exchange(send2, recv2, s2_s, s2_r, q, q + HALF, back=True)

    for load in loads[3:]:
        load.wait()
    near = run_expert(0)
    pair_begin(0)
    send_side(3)
    gather_end(1)
    reduce_begin(0)
    far = run_expert(1)
    pair_begin(1)
    reduce_middle(0)
    reduce_begin(1)

    stores = []

    def weight_gradient(n, ref, hbm, at, base):
        for f in range(4):
            ref[:, features(f)] = (
                mul_tn(near[at], unit_rows(base + f, 0)) + mul_tn(far[at], unit_rows(base + f, 1))
            ).astype(BF16)
        stores.append(pltpu.make_async_copy(ref, hbm.at[0], store_sem.at[n]))
        stores[-1].start()

    weight_gradient(0, gg_ref, gg_hbm, 1, 0)
    reduce_middle(1)
    reduce_end(0)
    weight_gradient(1, ug_ref, ug_hbm, 2, 0)
    weight_gradient(2, dg_ref, dg_hbm, 0, 4)
    reduce_end(1)

    arrived(side_recv, side_s, side_r, 0, PEERS)
    side_copy = remote(side_recv.at[:, :, LANE:], side_sib, pair_s.at[0], pair_r.at[0], at_expert(sibling))
    launch(side_copy)
    every = side_recv[...].reshape(PEERS * TOK, 2 * LANE)
    from_own = mul_tn(every[:, LANE:], every)
    side_copy.wait_recv()
    from_sib = mul_tn(side_sib[...].reshape(PEERS * TOK, LANE), every)
    for ref, mine_core, at in ((shared_gate_ref, 0, 0), (shared_up_ref, 0, UNITS), (shared_down_ref, 1, 2 * UNITS)):
        both = jnp.where(core == mine_core, from_own, from_sib)
        ref[...] = both[UNITS : UNITS + COLS, at : at + UNITS].astype(BF16)

    for copy in waits:
        copy.wait_send()
    waits.clear()
    sent(send1, s1_s, s1_r.at[0])
    sent(side_send, side_s, side_r)
    arrived(recv2, s2_s, s2_r, 0, PEERS)
    returned = recv2[...].reshape(rows, LANE)
    tokens = mul(back_hi_ref[...], returned) + mul(back_lo_ref[...], returned)
    shared_rows = jnp.concatenate(
        [final_ref[HALF_ROWS:, j * LANE : (j + 1) * LANE] for j in range(TILES)], axis=0
    )
    tok_ref[...] = tokens[: TILES * TOK] + shared_rows
    tok_copy = remote(tok_ref, tok_sib, pair_s.at[1], pair_r.at[1], at_expert(sibling))
    launch(tok_copy)
    tok_copy.wait_recv()
    summed = tok_ref[...] + tok_sib[...]
    full_ref[y] = summed.astype(BF16)
    for k in range(1, RING):
        other = ((y + k) % RING) * 2 + core
        launch(remote(full_ref.at[y], full_ref.at[y], e_s.at[k], e_r.at[k], at_expert(other)))

    terms = []
    for j in range(TILES):
        at = pl.ds(pl.multiple_of(quarter * QUARTER + j * LANE, LANE), LANE)
        terms.append(jnp.sum(summed[j * TOK : (j + 1) * TOK] * normalized_ref[:, at], axis=0, keepdims=True))
    line = jnp.concatenate(terms + [jnp.zeros((1, LANE), F32)], axis=1)
    for m in range(16):
        gain_send[m] = line[:, m * COLS : m * COLS + LANE]
    owner = (4 + x) * 2 + z // 8

    def gain_message(i):
        m = core * 8 + i
        peer = quarter * 16 + m
        return peer, remote(gain_send.at[m], gain_recv.at[(me + 2 * PEERS - 1 - peer) % PEERS], g_s.at[i], g_r, at_replica(peer))

    @pl.when(y >= 4)
    def send_gain():
        for i in range(8):
            peer, copy = gain_message(i)

            @pl.when(peer != me)
            def start():
                copy.start()

    @pl.when(expert == owner)
    def sum_gain():
        gain_recv[PEERS - 1] = gain_send[z]
        ref = gain_recv.at[: PEERS - 1]
        remote(ref, ref, g_s.at[0], g_r, at_replica((me + 1) % PEERS)).wait_recv()
        gain_all[...] = jnp.sum(gain_recv[...], axis=0)

        def tell(k, carry):
            other = (expert + k) % PARTS
            remote(gain_all, gain_all, gb_s.at[k], gb_r, at_expert(other)).start()
            return carry

        lax.fori_loop(1, PARTS, tell, 0)

    for k in range(1, RING):
        chip = (y + RING - k) % RING
        ref = full_ref.at[chip]
        remote(ref, ref, e_s.at[k], e_r.at[k], at_expert(chip * 2 + core)).wait_recv()

    def grad_tile(f, j):
        return full_ref[4 + f, j * TOK : (j + 1) * TOK, :].astype(F32)

    inner = jnp.zeros((TOK, LANE), F32)
    for f in range(4):
        for j in range(TILES):
            n = f * TILES + j
            inner = inner + grad_tile(f, j) * normalized_ref[:, feature_tile(f, j)] * gain_ref[n : n + 1, :]
    inner = jnp.sum(inner, axis=1, keepdims=True) * (1.0 / WIDTH)
    for f in range(4):
        for j in range(TILES):
            at, n = feature_tile(f, j), f * TILES + j
            moe_ref[:, at] = full_ref[f, j * TOK : (j + 1) * TOK, :]
            scaled = grad_tile(f, j) * gain_ref[n : n + 1, :]
            hidden_grad_ref[:, at] = (inv_rms * (scaled - normalized_ref[:, at] * inner)).astype(BF16)

    @pl.when(expert != owner)
    def take_gain():
        remote(gain_all, gain_all, gb_s.at[0], gb_r, at_expert(owner)).wait_recv()

    gain_grad_ref[...] = gain_all[...]

    for copy in waits:
        copy.wait_send()
    sent(send2, s2_s, s2_r)

    @pl.when(y >= 4)
    def gain_sent():
        for i in range(8):
            peer, copy = gain_message(i)

            @pl.when(peer != me)
            def wait():
                copy.wait_send()

    @pl.when(expert == owner)
    def told():
        def wait(k, carry):
            remote(gain_all, gain_all, gb_s.at[k], gb_r, at_expert((expert + k) % PARTS)).wait_send()
            return carry

        lax.fori_loop(1, PARTS, wait, 0)

    for store in stores:
        store.wait()


def hand_out(*refs):
    ins, outs, sems = refs[:9], refs[9:18], refs[18]
    copies = [pltpu.make_async_copy(src, dst, sems.at[n]) for n, (src, dst) in enumerate(zip(ins[:8], outs[:8]))]
    for copy in copies:
        copy.start()
    outs[8][...] = ins[8][0, :COLS]
    for copy in copies:
        copy.wait()


def per_device(
    hidden_in, norm_gain, expert_ids, gate_scores, w_gate, w_up, w_down, shared_gate, shared_up, shared_down, out_grad
):
    vmem, hbm = pl.BlockSpec(memory_space=pltpu.VMEM), pl.BlockSpec(memory_space=pl.ANY)
    dma = pltpu.SemaphoreType.DMA
    matrix = (UNITS, WIDTH)
    message = (PEERS, 16, LANE)
    tokens = jax.ShapeDtypeStruct((TOK, WIDTH), BF16)
    shared = jax.ShapeDtypeStruct((COLS, UNITS), BF16)
    weight = jax.ShapeDtypeStruct((1, UNITS, WIDTH), BF16)
    moe_out, hidden_grad, gain_grad, *grads = pl.pallas_call(
        layer_kernel,
        out_shape=(tokens, tokens, jax.ShapeDtypeStruct((1, LANE), F32), shared, shared, shared, weight, weight, weight),
        in_specs=[vmem] * 5 + [hbm] * 6,
        out_specs=[vmem] * 6 + [hbm] * 3,
        scratch_shapes=[pltpu.VMEM(matrix, BF16)] * 6
        + [
            dma((6,)),
            pltpu.VMEM((TOK, WIDTH), BF16),
            pltpu.VMEM((TOK, WIDTH), F32),
            pltpu.VMEM((LANE, PEERS * 16), BF16),
            pltpu.VMEM((LANE, PEERS * 16), BF16),
            pltpu.VMEM((TILES * SPAN, HALF * 16), BF16),
            pltpu.VMEM((HALF * 16, TILES * SPAN), BF16),
            pltpu.VMEM(message, BF16),
            pltpu.VMEM(message, BF16),
            pltpu.VMEM((RING, 2, HALF_ROWS, QUARTER), BF16),
            pltpu.VMEM((RING, 2, UNIT_ROWS, QUARTER), BF16),
            pltpu.VMEM((RING, UNIT_ROWS, QUARTER), BF16),
        ]
        + [pltpu.VMEM((4, UNIT_ROWS, QUARTER), BF16)] * 4
        + [
            pltpu.VMEM((UNIT_ROWS, QUARTER), F32),
            pltpu.VMEM((PEERS, TOK, 2 * LANE), BF16),
            pltpu.VMEM((PEERS, TOK, 2 * LANE), BF16),
            pltpu.VMEM((PEERS, TOK, LANE), BF16),
            pltpu.VMEM(message, BF16),
            pltpu.VMEM(message, BF16),
            pltpu.VMEM((TILES * TOK, LANE), F32),
            pltpu.VMEM((TILES * TOK, LANE), F32),
            pltpu.VMEM((RING, TILES * TOK, LANE), BF16),
            pltpu.VMEM((16, 1, LANE), F32),
            pltpu.VMEM((PEERS, 1, LANE), F32),
            pltpu.VMEM((1, LANE), F32),
        ]
        + [pltpu.VMEM(matrix, BF16)] * 3
        + [dma((3,))]
        + [dma, dma((2,)), dma, dma, dma, dma, dma((8,)), dma]
        + [dma((8,))] * 8
        + [dma((18,))] * 2
        + [dma((16,))] * 2
        + [dma((RING,))] * 2
        + [dma((PARTS,)), dma]
        + [dma((2,))] * 2,
        compiler_params=pltpu.CompilerParams(
            collective_id=0, has_side_effects=True, vmem_limit_bytes=56 * 1024 * 1024
        ),
    )(
        expert_ids.T,
        gate_scores.T,
        hidden_in,
        norm_gain.reshape(4 * TILES, LANE),
        out_grad,
        w_gate,
        w_up,
        w_down,
        shared_gate,
        shared_up,
        shared_down,
    )
    *copied, gain_grad = pl.pallas_call(
        hand_out,
        out_shape=(tokens, tokens, shared, shared, shared, weight, weight, weight, jax.ShapeDtypeStruct((COLS,), F32)),
        in_specs=[vmem] * 9,
        out_specs=[hbm] * 8 + [vmem],
        scratch_shapes=[dma((8,))],
    )(moe_out, hidden_grad, *grads, gain_grad)
    moe_out, hidden_grad, shared_gate_grad, shared_up_grad, shared_down_grad, *routed = copied
    return (
        moe_out, hidden_grad, gain_grad, *routed, shared_gate_grad.T, shared_up_grad.T, shared_down_grad.T
    )


def solution(mesh):
    rows, weights, shared = P("replica", None), P("replica", "expert", None), P("expert", None)
    return jax.shard_map(
        per_device,
        mesh=mesh,
        in_specs=(rows, P(), rows, rows, weights, weights, weights, shared, shared, shared, rows),
        out_specs=(rows, rows, P("replica"), weights, weights, weights) + (P("expert", "replica"),) * 3,
        check_vma=False,
    )
```
